32 devices in a mesh: seq: 4 (over y, x), dp: 8 (over z, core).
Axes of the slice: x: 2, y: 2, z: 4, core: 2. Of those that a mesh axis runs over, the one named last changes fastest.
Arguments:
- queries: bfloat16 [8, 512, 2048], P('dp', 'seq'), may hold values from -6 to 6
- key_rows: bfloat16 [8, 512, 2048], P('dp', 'seq'), may hold values from -6 to 6
- values: bfloat16 [8, 512, 2048], P('dp', 'seq'), may hold values from -6 to 6
- cotangent: bfloat16 [8, 512, 2048], P('dp', 'seq'), may hold values from -6 to 6
- slice_ids: int32 [8, 512], P('dp', 'seq'), may hold values from 0 to 1, never falling along the last dimension, each value on 1 to 400 neighbouring positions
- query_gain: float32 [128], replicated, may hold values from 0.1 to 1.9
- key_gain: float32 [128], replicated, may hold values from 0.1 to 1.9
Outputs:
- attended: bfloat16 [8, 512, 2048], P('dp', 'seq')
- query_grad: bfloat16 [8, 512, 2048], P('dp', 'seq')
- key_grad: bfloat16 [8, 512, 2048], P('dp', 'seq')
- value_grad: bfloat16 [8, 512, 2048], P('dp', 'seq')
- query_gain_grad: float32 [128], replicated
- key_gain_grad: float32 [128], replicated
The draws below stay inside these ranges and needn't reach their ends.
Inputs may be any that keep to these rules, and one draw needn't show every extreme that they name: `slice_ids`: within each packed sequence the slice numbers never fall, and each slice holds 1 to 400 rows.
All inputs are finite; a program needn't handle non-finite values.
Results may differ from the reference program's by a relative error of at most 0.0086.
Values may be sent and summed in bfloat16 or wider, within the bound.
No kernel may reach another device: no remote copies, remote signals or barrier semaphores. Data moves between devices by JAX's collectives and lax.ppermute only.
A program may use at most 64 MiB of HBM per device.

```python
import math
import jax
import jax.numpy as jnp
import numpy as np
from jax import lax

HEADS = 16
HEAD_DIM = 128
D = 2048
SLICES = 2
LENGTH = 512
SLICE_MOST = 400
BATCH = 8


def steps_of(own_key, shape, pieces, low, high):
    def one(position, blocks):
        draws = jax.random.uniform(jax.random.fold_in(jax.random.fold_in(own_key, 6), position), (blocks,), jnp.float32, low / len(pieces), high / len(pieces))
        return jnp.repeat(jnp.exp(draws), shape[position] // blocks).reshape((-1,) + (1,) * (len(shape) - position - 1))

    level = one(*pieces[0])
    for cut in pieces[1:]:
        level = level * one(*cut)
    return level


def length_profile(number_of, total, bound, lean):
    weights = [(1 << 20) // math.isqrt(grade ** lean) + 1 for grade in range(2, number_of + 1)]
    rest, counts = total - bound - (number_of - 1), [1] * (number_of - 1)
    while rest > 0:
        movable = [i for i in range(number_of - 1) if counts[i] < bound]
        whole, remaining = sum([weights[i] for i in movable]), rest
        for i in movable:
            more = min(bound - counts[i], max(1, remaining * weights[i] // whole), rest)
            counts[i] = counts[i] + more
            rest = rest - more
    return np.array([bound] + counts)


def ragged_sizes(rng, amount, total, limit, lean):
    if amount == 2:
        one = jax.random.randint(rng, (), max(1, total - limit), min(limit, total - 1) + 1)
        return jnp.stack([one, total - one])
    sizes = jnp.asarray(length_profile(amount, total, limit, lean), jnp.int32)
    pairs = (amount - 1) // 2
    giver, sink = sizes[1:1 + 2 * pairs:2], sizes[2:2 + 2 * pairs:2]
    slack = jnp.minimum(giver - 1, limit - sink)
    shifted = jax.random.randint(jax.random.fold_in(rng, 1), (pairs,), 0, 1 << 20) % (slack + 1)
    sizes = sizes.at[1:1 + 2 * pairs:2].set(giver - shifted).at[2:2 + 2 * pairs:2].set(sink + shifted)
    return sizes[jax.random.permutation(jax.random.fold_in(rng, 2), amount)]


def bell_draw(stream_key, dims, spread, most, cuts=(), dtype=jnp.bfloat16):
    factor_of = steps_of(stream_key, dims, cuts, -0.22, 0.18) if cuts else 1.0
    array = jax.random.normal(stream_key, dims, jnp.float32) * spread * factor_of
    return jnp.minimum(jnp.maximum(array, -most), most).astype(dtype)


def setup_inputs(seed: int = 0) -> dict:
    splits = jax.random.split(jax.random.key(seed), 8)
    return {
        "queries": bell_draw(splits[0], (BATCH, LENGTH, D), 1.0, 6.0, ((0, 8), (1, 4))),
        "key_rows": bell_draw(splits[1], (BATCH, LENGTH, D), 1.0, 6.0, ((0, 8), (1, 4))),
        "values": bell_draw(splits[2], (BATCH, LENGTH, D), 1.0, 6.0, ((0, 8), (1, 4))),
        "cotangent": bell_draw(splits[3], (BATCH, LENGTH, D), 1.0, 6.0, ((0, 8), (1, 4))),
        "slice_ids": jax.vmap(lambda own: jnp.searchsorted(jnp.cumsum(ragged_sizes(own, SLICES, LENGTH, SLICE_MOST, 1)), jnp.arange(LENGTH), side="right"))(jax.random.split(splits[4], BATCH)).reshape((BATCH, LENGTH)).astype(jnp.int32),
        "query_gain": jnp.clip(1.0 + 0.18 * jax.random.normal(splits[5], (HEAD_DIM,), jnp.float32), 0.1, 1.9),
        "key_gain": jnp.clip(1.0 + 0.18 * jax.random.normal(splits[6], (HEAD_DIM,), jnp.float32), 0.1, 1.9),
    }


def normalize(rows, gain):
    floats = rows.astype(jnp.float32)
    inv_rms = lax.rsqrt(lax.optimization_barrier(jnp.mean(floats * floats, axis=-1, keepdims=True)) + 1e-06)
    normed = floats * inv_rms
    return (normed, inv_rms, (normed * gain).astype(jnp.bfloat16))

def norm_back(grad_out, normed, inv_rms, gain):
    grad_normed = grad_out * gain
    inner_mean = lax.optimization_barrier(jnp.mean(grad_normed * normed, axis=-1, keepdims=True))
    grad_rows = (inv_rms * (grad_normed - normed * inner_mean)).astype(jnp.bfloat16)
    return (grad_rows, lax.optimization_barrier(jnp.sum(grad_out * normed, axis=0)))

def attend_head(queries, key_rows, values, cotangent, slice_ids, query_gain, key_gain):
    length = queries.shape[0]
    block_rows = math.gcd(length, 512)
    blocks_count = length // block_rows
    score_scale = HEAD_DIM ** (-0.5)
    q_normed, q_inv, q_ready = normalize(queries, query_gain)
    k_normed, k_inv, k_ready = normalize(key_rows, key_gain)

    def one_block(carry, inputs):
        value_acc, key_acc = carry
        q_block, grad_block, ids_block = inputs
        scores = jnp.dot(q_block, k_ready.T, preferred_element_type=jnp.float32) * score_scale
        same = ids_block[:, None] == slice_ids[None, :]
        weights = jnp.where(same, jnp.exp(scores), jnp.zeros_like(scores))
        probs = weights / lax.optimization_barrier(jnp.sum(weights, axis=1, keepdims=True))
        probs_low = probs.astype(jnp.bfloat16)
        attended = jnp.dot(probs_low, values, preferred_element_type=jnp.float32).astype(jnp.bfloat16)
        row_inner = lax.optimization_barrier(jnp.sum(grad_block.astype(jnp.float32) * attended.astype(jnp.float32), axis=1, keepdims=True))
        grad_probs = jnp.dot(grad_block, values.T, preferred_element_type=jnp.float32)
        grad_scores = (probs * (grad_probs - row_inner) * score_scale).astype(jnp.bfloat16)
        value_acc = value_acc + jnp.dot(probs_low.T, grad_block, preferred_element_type=jnp.float32)
        key_acc = key_acc + jnp.dot(grad_scores.T, q_block, preferred_element_type=jnp.float32)
        query_part = jnp.dot(grad_scores, k_ready, preferred_element_type=jnp.float32)
        return ((value_acc, key_acc), (attended, query_part))
    zeros = jnp.zeros((length, queries.shape[1]), jnp.float32)
    inputs = (q_ready.reshape(blocks_count, block_rows, -1), cotangent.reshape(blocks_count, block_rows, -1), slice_ids.reshape(blocks_count, block_rows))
    (value_acc, key_acc), (attended, query_part) = lax.scan(one_block, (zeros, zeros), inputs)
    attended = attended.reshape(length, -1)
    query_part = query_part.reshape(length, -1)
    query_grad, q_gain_part = norm_back(query_part, q_normed, q_inv, query_gain)
    key_grad, k_gain_part = norm_back(key_acc, k_normed, k_inv, key_gain)
    return (attended, query_grad, key_grad, value_acc.astype(jnp.bfloat16), q_gain_part, k_gain_part)

def reference(queries, key_rows, values, cotangent, slice_ids, query_gain, key_gain):
    batch, length, width = queries.shape

    def heads_first(tensor):
        return tensor.reshape(batch, length, HEADS, HEAD_DIM).transpose(0, 2, 1, 3).reshape(batch * HEADS, length, HEAD_DIM)

    def rows_first(tensor):
        return tensor.reshape(batch, HEADS, length, HEAD_DIM).transpose(0, 2, 1, 3).reshape(batch, length, width)
    repeated = jnp.repeat(slice_ids, HEADS, axis=0)

    def run(items):
        return attend_head(items[0], items[1], items[2], items[3], items[4], query_gain, key_gain)
    results = lax.map(run, (heads_first(queries), heads_first(key_rows), heads_first(values), heads_first(cotangent), repeated))
    return (rows_first(results[0]), rows_first(results[1]), rows_first(results[2]), rows_first(results[3]), lax.optimization_barrier(jnp.sum(results[4], axis=0)), lax.optimization_barrier(jnp.sum(results[5], axis=0)))
```

```python
import functools

import jax
import jax.numpy as jnp
from jax import lax
from jax.experimental import pallas as pl
from jax.experimental.pallas import tpu as pltpu
from jax.sharding import PartitionSpec as P

HEAD_DIM = 128
EPS = 1e-06
TENSORS = 4
ID_ROWS = 16
SCALE = HEAD_DIM ** (-0.5)
VMEM_BYTES = 56 * 1024 * 1024


def dot(a, b, contract):
    return lax.dot_general(
        a, b, ((contract[:1], contract[1:]), ((), ())), preferred_element_type=jnp.float32
    )


def normalize(rows, gain):
    floats = rows.astype(jnp.float32)
    inv_rms = lax.rsqrt(jnp.mean(floats * floats, axis=-1, keepdims=True) + EPS)
    normed = floats * inv_rms
    return normed, inv_rms, (normed * gain).astype(jnp.bfloat16)


def norm_back(grad_out, normed, inv_rms, gain):
    grad_normed = grad_out * gain
    inner_mean = jnp.mean(grad_normed * normed, axis=-1, keepdims=True)
    grad_rows = (inv_rms * (grad_normed - normed * inner_mean)).astype(jnp.bfloat16)
    return grad_rows, jnp.sum(grad_out * normed, axis=0, keepdims=True)


def pack_kernel(groups, local, chunk, width, with_ids, me_ref, *refs):
    tensors, rest = refs[:TENSORS], refs[TENSORS:]
    if with_ids:
        ids_ref, rest = rest[0], rest[1:]
    outs, sems = rest[:groups], rest[groups]
    rows = tensors[0].shape[1]
    copies = []
    for shift in range(groups):
        owner = jnp.bitwise_xor(me_ref[0], shift)
        start = pl.multiple_of(owner * local + chunk * width, HEAD_DIM)
        for t in range(TENSORS):
            copies.append((
                tensors[t].at[0, :, pl.ds(start, width)],
                outs[shift].at[pl.ds(t * rows, rows), :],
            ))
        if with_ids:
            copies.append((ids_ref, outs[shift].at[pl.ds(TENSORS * rows, ID_ROWS), :]))
    started = [
        pltpu.make_async_copy(source, target, sems.at[i])
        for i, (source, target) in enumerate(copies)
    ]
    for copy in started:
        copy.start()
    for copy in started:
        copy.wait()


def pack(me, arrays, ids_block, groups, local, chunk, width):
    rows = arrays[0].shape[1]
    with_ids = ids_block is not None
    height = TENSORS * rows + (ID_ROWS if with_ids else 0)
    count = groups * (TENSORS + (1 if with_ids else 0))
    any_spec = pl.BlockSpec(memory_space=pl.ANY)
    operands = (me,) + tuple(arrays) + ((ids_block,) if with_ids else ())
    return pl.pallas_call(
        functools.partial(pack_kernel, groups, local, chunk, width, with_ids),
        out_shape=[jax.ShapeDtypeStruct((height, width), jnp.bfloat16)] * groups,
        in_specs=[pl.BlockSpec(memory_space=pltpu.SMEM)] + [any_spec] * (len(operands) - 1),
        out_specs=[any_spec] * groups,
        scratch_shapes=[pltpu.SemaphoreType.DMA((count,))],
        name=f"pack{chunk}",
    )(*operands)


def unpack_kernel(groups, local, chunk, width, aliased, me_ref, *refs):
    pieces, rest = refs[:groups], refs[groups:]
    if aliased:
        rest = rest[TENSORS:]
    outs, sems = rest[:TENSORS], rest[TENSORS]
    rows = outs[0].shape[1]
    started = []
    for shift in range(groups):
        owner = jnp.bitwise_xor(me_ref[0], shift)
        start = pl.multiple_of(owner * local + chunk * width, HEAD_DIM)
        for t in range(TENSORS):
            started.append(
                pltpu.make_async_copy(
                    pieces[shift].at[pl.ds(t * rows, rows), :],
                    outs[t].at[0, :, pl.ds(start, width)],
                    sems.at[shift * TENSORS + t],
                )
            )
    for copy in started:
        copy.start()
    for copy in started:
        copy.wait()


def unpack(me, pieces, previous, shape, local, chunk, width):
    groups = len(pieces)
    aliased = previous is not None
    any_spec = pl.BlockSpec(memory_space=pl.ANY)
    operands = (me,) + tuple(pieces) + (tuple(previous) if aliased else ())
    aliases = {1 + groups + t: t for t in range(TENSORS)} if aliased else {}
    return pl.pallas_call(
        functools.partial(unpack_kernel, groups, local, chunk, width, aliased),
        out_shape=[jax.ShapeDtypeStruct(shape, jnp.bfloat16)] * TENSORS,
        in_specs=[pl.BlockSpec(memory_space=pltpu.SMEM)] + [any_spec] * (len(operands) - 1),
        out_specs=[any_spec] * TENSORS,
        scratch_shapes=[pltpu.SemaphoreType.DMA((groups * TENSORS,))],
        input_output_aliases=aliases,
        name=f"unpack{chunk}",
    )(*operands)


def attend_kernel(groups, rows, heads, block, *refs):
    pieces, ids, rest = refs[:groups], refs[groups : 2 * groups], refs[2 * groups :]
    gain_refs, outs, gain_out = rest[:2], rest[2 : 2 + groups], rest[2 + groups]
    length = groups * rows
    query_gain, key_gain = gain_refs[0][...], gain_refs[1][...]
    ids_row = jnp.concatenate([ref[0:1, 0:rows].astype(jnp.float32) for ref in ids], axis=1)
    ids_col = jnp.broadcast_to(ids_row, (HEAD_DIM, length)).T[:, 0:1]
    gain_parts = [jnp.zeros((1, HEAD_DIM), jnp.float32)] * 2
    for head in range(heads):
        cols = slice(head * HEAD_DIM, (head + 1) * HEAD_DIM)

        def gather(t):
            return jnp.concatenate(
                [ref[t * rows : (t + 1) * rows, cols] for ref in pieces], axis=0
            )

        q_normed, q_inv, q_ready = normalize(gather(0), query_gain)
        k_normed, k_inv, k_ready = normalize(gather(1), key_gain)
        values, cotangent = gather(2), gather(3)
        value_acc = key_acc = None
        attended_parts, query_parts = [], []
        for start in range(0, length, block):
            part = slice(start, start + block)
            q_block, grad_block = q_ready[part], cotangent[part]
            scores = dot(q_block, k_ready, (1, 1)) * SCALE
            weights = jnp.where(ids_col[part] == ids_row, jnp.exp(scores), 0.0)
            probs = weights * (1.0 / jnp.sum(weights, axis=1, keepdims=True))
            probs_low = probs.astype(jnp.bfloat16)
            attended = dot(probs_low, values, (1, 0)).astype(jnp.bfloat16)
            row_inner = jnp.sum(
                grad_block.astype(jnp.float32) * attended.astype(jnp.float32),
                axis=1,
                keepdims=True,
            )
            grad_probs = dot(grad_block, values, (1, 1))
            grad_scores = (probs * (grad_probs - row_inner) * SCALE).astype(jnp.bfloat16)
            value_part = dot(probs_low, grad_block, (0, 0))
            key_part = dot(grad_scores, q_block, (0, 0))
            value_acc = value_part if value_acc is None else value_acc + value_part
            key_acc = key_part if key_acc is None else key_acc + key_part
            attended_parts.append(attended)
            query_parts.append(dot(grad_scores, k_ready, (1, 0)))
        attended = jnp.concatenate(attended_parts, axis=0)
        query_acc = jnp.concatenate(query_parts, axis=0)
        query_grad, query_sum = norm_back(query_acc, q_normed, q_inv, query_gain)
        key_grad, key_sum = norm_back(key_acc, k_normed, k_inv, key_gain)
        gain_parts = [gain_parts[0] + query_sum, gain_parts[1] + key_sum]
        results = (attended, query_grad, key_grad, value_acc.astype(jnp.bfloat16))
        for i, out in enumerate(outs):
            for t in range(TENSORS):
                out[t * rows : (t + 1) * rows, cols] = results[t][i * rows : (i + 1) * rows]
    gain_out[0:1, :] = gain_parts[0]
    gain_out[1:2, :] = gain_parts[1]


def attend(pieces, id_holders, query_gain, key_gain, rows, heads, chunk):
    groups = len(pieces)
    width = heads * HEAD_DIM
    length = groups * rows
    height = TENSORS * rows
    block = min(length, 256)
    piece_spec = pl.BlockSpec((height, width), lambda i: (0, 0))
    ids_spec = pl.BlockSpec((ID_ROWS, HEAD_DIM), lambda i: (height // ID_ROWS, 0))
    gain_spec = pl.BlockSpec((1, HEAD_DIM), lambda i: (0, 0))
    area = length * length * heads
    outs = pl.pallas_call(
        functools.partial(attend_kernel, groups, rows, heads, block),
        grid=(1,),
        out_shape=[jax.ShapeDtypeStruct((height, width), jnp.bfloat16)] * groups
        + [jax.ShapeDtypeStruct((2, HEAD_DIM), jnp.float32)],
        in_specs=[piece_spec] * groups + [ids_spec] * groups + [gain_spec] * 2,
        out_specs=[piece_spec] * groups + [pl.BlockSpec((2, HEAD_DIM), lambda i: (0, 0))],
        compiler_params=pltpu.CompilerParams(vmem_limit_bytes=VMEM_BYTES),
        cost_estimate=pl.CostEstimate(
            flops=12 * area * HEAD_DIM,
            bytes_accessed=4 * groups * height * width,
            transcendentals=area,
        ),
        name=f"attend{chunk}",
    )(*pieces, *id_holders, query_gain, key_gain)
    return outs[:groups], outs[groups]


def permute(value, axis, size, shift):
    return lax.ppermute(value, axis, [(i, i ^ shift) for i in range(size)])


def total_over(value, axis, size):
    shift = 1
    while shift < size:
        value = value + permute(value, axis, size, shift)
        shift *= 2
    return value


def per_device(queries, key_rows, values, cotangent, slice_ids, query_gain, key_gain):
    rows, width = queries.shape[1], queries.shape[2]
    groups, batches = lax.axis_size("seq"), lax.axis_size("dp")
    local = width // groups
    chunks = 2 if local >= 2 * HEAD_DIM else 1
    chunk_width = local // chunks
    heads = chunk_width // HEAD_DIM
    me = lax.axis_index("seq").astype(jnp.int32).reshape(1)
    arrays = (queries, key_rows, values, cotangent)
    ids_block = jnp.pad(
        slice_ids.astype(jnp.bfloat16), ((0, ID_ROWS - 1), (0, chunk_width - rows))
    )
    gains = (query_gain.reshape(1, HEAD_DIM), key_gain.reshape(1, HEAD_DIM))

    received = []
    for chunk in range(chunks):
        payloads = pack(
            me, arrays, ids_block if chunk == 0 else None, groups, local, chunk, chunk_width
        )
        received.append(
            [payloads[0]]
            + [permute(payloads[shift], "seq", groups, shift) for shift in range(1, groups)]
        )
    returned, gain_total = [], None
    for chunk in range(chunks):
        results, gain_part = attend(
            received[chunk], received[0], gains[0], gains[1], rows, heads, chunk
        )
        gain_total = gain_part if gain_total is None else gain_total + gain_part
        returned.append(
            [results[0]]
            + [permute(results[shift], "seq", groups, shift) for shift in range(1, groups)]
        )
    gain_total = total_over(gain_total, "dp", batches)
    gain_total = total_over(gain_total, "seq", groups)
    outputs = None
    for chunk in range(chunks):
        outputs = unpack(me, returned[chunk], outputs, queries.shape, local, chunk, chunk_width)
    return (*outputs, gain_total[0], gain_total[1])


def solution(mesh):
    rows = P("dp", "seq", None)
    return jax.shard_map(
        per_device,
        mesh=mesh,
        in_specs=(rows, rows, rows, rows, P("dp", "seq"), P(), P()),
        out_specs=(rows, rows, rows, rows, P(), P()),
        check_vma=False,
    )
```

```python
import functools

import jax
import jax.numpy as jnp
from jax import lax
from jax.experimental import pallas as pl
from jax.experimental.pallas import tpu as pltpu
from jax.sharding import PartitionSpec as P

HEAD_DIM = 128
EPS = 1e-06
TENSORS = 4
ID_ROWS = 16
SCALE = HEAD_DIM ** (-0.5)
MIB = 1024 * 1024


def dot(a, b, contract):
    return lax.dot_general(
        a, b, ((contract[:1], contract[1:]), ((), ())), preferred_element_type=jnp.float32
    )


def normalize(rows, gain):
    floats = rows.astype(jnp.float32)
    inv_rms = lax.rsqrt(jnp.mean(floats * floats, axis=-1, keepdims=True) + EPS)
    normed = floats * inv_rms
    return normed, inv_rms, (normed * gain).astype(jnp.bfloat16)


def norm_back(grad_out, normed, inv_rms, gain):
    grad_normed = grad_out * gain
    inner_mean = jnp.mean(grad_normed * normed, axis=-1, keepdims=True)
    grad_rows = (inv_rms * (grad_normed - normed * inner_mean)).astype(jnp.bfloat16)
    return grad_rows, jnp.sum(grad_out * normed, axis=0, keepdims=True)


def pack_kernel(groups, local, chunk, width, with_ids, *refs):
    tensors, rest = refs[:TENSORS], refs[TENSORS:]
    if with_ids:
        ids_ref, rest = rest[0], rest[1:]
    outs, sems = rest[:groups], rest[groups]
    rows = tensors[0].shape[1]
    started = []
    for shift in range(groups):
        owner = jnp.bitwise_xor(lax.axis_index("seq"), shift)
        start = pl.multiple_of(owner * local + chunk * width, HEAD_DIM)
        for t in range(TENSORS):
            started.append(
                pltpu.make_async_copy(
                    tensors[t].at[0, :, pl.ds(start, width)],
                    outs[shift].at[pl.ds(t * rows, rows), :],
                    sems.at[shift * TENSORS + t],
                )
            )
    for copy in started:
        copy.start()
    if with_ids:
        ids = jnp.broadcast_to(ids_ref[...].astype(jnp.float32), (ID_ROWS, rows))
        for out in outs:
            for first in range(0, width, rows):
                out[TENSORS * rows :, first : first + rows] = ids.astype(jnp.bfloat16)
    for copy in started:
        copy.wait()


def pack(arrays, slice_ids, groups, local, chunk, width):
    rows = arrays[0].shape[1]
    with_ids = slice_ids is not None
    height = TENSORS * rows + (ID_ROWS if with_ids else 0)
    vmem_spec = pl.BlockSpec(memory_space=pltpu.VMEM)
    operands = tuple(arrays) + ((slice_ids,) if with_ids else ())
    return pl.pallas_call(
        functools.partial(pack_kernel, groups, local, chunk, width, with_ids),
        out_shape=[jax.ShapeDtypeStruct((height, width), jnp.bfloat16)] * groups,
        in_specs=[pl.BlockSpec(memory_space=pltpu.HBM)] * TENSORS
        + [vmem_spec] * (len(operands) - TENSORS),
        out_specs=[vmem_spec] * groups,
        scratch_shapes=[pltpu.SemaphoreType.DMA((TENSORS * groups,))],
        compiler_params=pltpu.CompilerParams(vmem_limit_bytes=8 * MIB),
        name=f"pack{chunk}",
    )(*operands)


def unpack_kernel(groups, local, chunk, width, aliased, carries, *refs):
    pieces, rest = refs[:groups], refs[groups:]
    if aliased:
        rest = rest[TENSORS:]
    if carries:
        rest[TENSORS + 1][...] = rest[0][...]
        rest = rest[1 : TENSORS + 1] + rest[TENSORS + 2 :]
    outs, sems = rest[:TENSORS], rest[TENSORS]
    rows = outs[0].shape[1]
    started = []
    for shift in range(groups):
        owner = jnp.bitwise_xor(lax.axis_index("seq"), shift)
        start = pl.multiple_of(owner * local + chunk * width, HEAD_DIM)
        for t in range(TENSORS):
            started.append(
                pltpu.make_async_copy(
                    pieces[shift].at[pl.ds(t * rows, rows), :],
                    outs[t].at[0, :, pl.ds(start, width)],
                    sems.at[shift * TENSORS + t],
                )
            )
    for copy in started:
        copy.start()
    for copy in started:
        copy.wait()


def unpack(pieces, previous, carried, shape, local, chunk, width):
    groups = len(pieces)
    aliased, carries = previous is not None, carried is not None
    any_spec = pl.BlockSpec(memory_space=pltpu.HBM)
    vmem_spec = pl.BlockSpec(memory_space=pltpu.VMEM)
    operands = tuple(pieces) + (tuple(previous) if aliased else ())
    aliases = {groups + t: t for t in range(TENSORS)} if aliased else {}
    extra = ([carried], [vmem_spec]) if carries else ([], [])
    return pl.pallas_call(
        functools.partial(unpack_kernel, groups, local, chunk, width, aliased, carries),
        out_shape=[jax.ShapeDtypeStruct(shape, jnp.bfloat16)] * TENSORS
        + [jax.ShapeDtypeStruct(value.shape, value.dtype) for value in extra[0]],
        in_specs=[vmem_spec] * groups + [any_spec] * (len(operands) - groups) + extra[1],
        out_specs=[any_spec] * TENSORS + extra[1],
        scratch_shapes=[pltpu.SemaphoreType.DMA((groups * TENSORS,))],
        input_output_aliases=aliases,
        compiler_params=pltpu.CompilerParams(vmem_limit_bytes=8 * MIB),
        name=f"unpack{chunk}",
    )(*operands, *extra[0])


def attend_kernel(groups, rows, heads, block, *refs):
    pieces, ids, rest = refs[:groups], refs[groups : 2 * groups], refs[2 * groups :]
    gain_refs, outs, gain_out = rest[:2], rest[2 : 2 + groups], rest[2 + groups]
    length = groups * rows
    query_gain, key_gain = gain_refs[0][...], gain_refs[1][...]
    ids_row = jnp.concatenate([ref[0:1, 0:rows].astype(jnp.float32) for ref in ids], axis=1)
    ids_col = jnp.broadcast_to(ids_row, (HEAD_DIM, length)).T[:, 0:1]
    gain_parts = [jnp.zeros((1, HEAD_DIM), jnp.float32)] * 2
    for head in range(heads):
        cols = slice(head * HEAD_DIM, (head + 1) * HEAD_DIM)

        def gather(t):
            return jnp.concatenate(
                [ref[t * rows : (t + 1) * rows, cols] for ref in pieces], axis=0
            )

        q_normed, q_inv, q_ready = normalize(gather(0), query_gain)
        k_normed, k_inv, k_ready = normalize(gather(1), key_gain)
        values, cotangent = gather(2), gather(3)
        value_acc = key_acc = None
        attended_parts, query_parts = [], []
        for start in range(0, length, block):
            part = slice(start, start + block)
            q_block, grad_block = q_ready[part], cotangent[part]
            scores = dot(q_block, k_ready, (1, 1)) * SCALE
            weights = jnp.where(ids_col[part] == ids_row, jnp.exp(scores), 0.0)
            probs = weights * (1.0 / jnp.sum(weights, axis=1, keepdims=True))
            probs_low = probs.astype(jnp.bfloat16)
            attended = dot(probs_low, values, (1, 0)).astype(jnp.bfloat16)
            row_inner = jnp.sum(
                grad_block.astype(jnp.float32) * attended.astype(jnp.float32),
                axis=1,
                keepdims=True,
            )
            grad_probs = dot(grad_block, values, (1, 1))
            grad_scores = (probs * (grad_probs - row_inner) * SCALE).astype(jnp.bfloat16)
            value_part = dot(probs_low, grad_block, (0, 0))
            key_part = dot(grad_scores, q_block, (0, 0))
            value_acc = value_part if value_acc is None else value_acc + value_part
            key_acc = key_part if key_acc is None else key_acc + key_part
            attended_parts.append(attended)
            query_parts.append(dot(grad_scores, k_ready, (1, 0)))
        attended = jnp.concatenate(attended_parts, axis=0)
        query_acc = jnp.concatenate(query_parts, axis=0)
        query_grad, query_sum = norm_back(query_acc, q_normed, q_inv, query_gain)
        key_grad, key_sum = norm_back(key_acc, k_normed, k_inv, key_gain)
        gain_parts = [gain_parts[0] + query_sum, gain_parts[1] + key_sum]
        results = (attended, query_grad, key_grad, value_acc.astype(jnp.bfloat16))
        for i, out in enumerate(outs):
            for t in range(TENSORS):
                out[t * rows : (t + 1) * rows, cols] = results[t][i * rows : (i + 1) * rows]
    gain_out[0:1, :] = gain_parts[0]
    gain_out[1:2, :] = gain_parts[1]


def attend(pieces, id_holders, query_gain, key_gain, rows, heads, chunk):
    groups = len(pieces)
    width = heads * HEAD_DIM
    length = groups * rows
    height = TENSORS * rows
    block = min(length, 256)
    piece_spec = pl.BlockSpec((height, width), lambda i: (0, 0))
    ids_spec = pl.BlockSpec((ID_ROWS, HEAD_DIM), lambda i: (height // ID_ROWS, 0))
    gain_spec = pl.BlockSpec((1, HEAD_DIM), lambda i: (0, 0))
    area = length * length * heads
    outs = pl.pallas_call(
        functools.partial(attend_kernel, groups, rows, heads, block),
        grid=(1,),
        out_shape=[jax.ShapeDtypeStruct((height, width), jnp.bfloat16)] * groups
        + [jax.ShapeDtypeStruct((2, HEAD_DIM), jnp.float32)],
        in_specs=[piece_spec] * groups + [ids_spec] * groups + [gain_spec] * 2,
        out_specs=[piece_spec] * groups + [pl.BlockSpec((2, HEAD_DIM), lambda i: (0, 0))],
        compiler_params=pltpu.CompilerParams(vmem_limit_bytes=(24 if length <= 512 else 48) * MIB),
        cost_estimate=pl.CostEstimate(
            flops=12 * area * HEAD_DIM,
            bytes_accessed=4 * groups * height * width,
            transcendentals=area,
        ),
        name=f"attend{chunk}",
    )(*pieces, *id_holders, query_gain, key_gain)
    return outs[:groups], outs[groups]


def permute(value, axis, size, shift):
    return lax.ppermute(value, axis, [(i, i ^ shift) for i in range(size)])


def total_over(value, axis, size):
    shift = 1
    while shift < size:
        value = value + permute(value, axis, size, shift)
        shift *= 2
    return value


def per_device(queries, key_rows, values, cotangent, slice_ids, query_gain, key_gain):
    rows, width = queries.shape[1], queries.shape[2]
    groups, batches = lax.axis_size("seq"), lax.axis_size("dp")
    local = width // groups
    chunks = 2 if local >= 2 * HEAD_DIM else 1
    chunk_width = local // chunks
    heads = chunk_width // HEAD_DIM
    arrays = (queries, key_rows, values, cotangent)
    gains = (query_gain.reshape(1, HEAD_DIM), key_gain.reshape(1, HEAD_DIM))

    received = []
    for chunk in range(chunks):
        payloads = pack(
            arrays, slice_ids if chunk == 0 else None, groups, local, chunk, chunk_width
        )
        received.append(
            [payloads[0]]
            + [permute(payloads[shift], "seq", groups, shift) for shift in range(1, groups)]
        )
    returned, gain_total = [], None
    for chunk in range(chunks):
        results, gain_part = attend(
            received[chunk], received[0], gains[0], gains[1], rows, heads, chunk
        )
        gain_total = gain_part if gain_total is None else gain_total + gain_part
        returned.append(
            [results[0]]
            + [permute(results[shift], "seq", groups, shift) for shift in range(1, groups)]
        )
    outputs = None
    for chunk in range(chunks):
        carried = gain_total if chunk == 0 else None
        outputs = unpack(
            returned[chunk], outputs, carried, queries.shape, local, chunk, chunk_width
        )
        if chunk == 0:
            *outputs, gain_total = outputs
    gain_total = total_over(gain_total, "dp", batches)
    gain_total = total_over(gain_total, "seq", groups)
    return (*outputs, gain_total[0], gain_total[1])


def solution(mesh):
    rows = P("dp", "seq", None)
    return jax.shard_map(
        per_device,
        mesh=mesh,
        in_specs=(rows, rows, rows, rows, P("dp", "seq"), P(), P()),
        out_specs=(rows, rows, rows, rows, P(), P()),
        check_vma=False,
    )
```

```python
import functools

import jax
import jax.numpy as jnp
from jax import lax
from jax.experimental import pallas as pl
from jax.experimental.pallas import tpu as pltpu
from jax.sharding import PartitionSpec as P

HEAD_DIM = 128
EPS = 1e-06
TENSORS = 4
ID_ROWS = 16
SCALE = HEAD_DIM ** (-0.5)
MIB = 1024 * 1024
PACK_MIB = 58


def dot(a, b, contract):
    return lax.dot_general(
        a, b, ((contract[:1], contract[1:]), ((), ())), preferred_element_type=jnp.float32
    )


def normalize(rows, gain):
    floats = rows.astype(jnp.float32)
    inv_rms = lax.rsqrt(jnp.mean(floats * floats, axis=-1, keepdims=True) + EPS)
    normed = floats * inv_rms
    return normed, inv_rms, (normed * gain).astype(jnp.bfloat16)


def norm_back(grad_out, normed, inv_rms, gain):
    grad_normed = grad_out * gain
    inner_mean = jnp.mean(grad_normed * normed, axis=-1, keepdims=True)
    grad_rows = (inv_rms * (grad_normed - normed * inner_mean)).astype(jnp.bfloat16)
    return grad_rows, jnp.sum(grad_out * normed, axis=0, keepdims=True)


def pack_kernel(groups, local, chunk, width, first, *refs):
    tensors, rest = refs[:TENSORS], refs[TENSORS:]
    if first:
        (ids_ref, *gain_refs), rest = rest[:3], rest[3:]
    outs, rest = rest[:groups], rest[groups:]
    if first:
        gain_outs, rest = rest[:2], rest[2:]
    sems = rest[0]
    rows = tensors[0].shape[1]
    pairs = []
    if first:
        pairs.append((ids_ref, rest[1]))
        pairs.extend(zip(gain_refs, gain_outs))
    for shift in range(groups):
        owner = jnp.bitwise_xor(lax.axis_index("seq"), shift)
        start = pl.multiple_of(owner * local + chunk * width, HEAD_DIM)
        for t in range(TENSORS):
            pairs.append((
                tensors[t].at[0, :, pl.ds(start, width)],
                outs[shift].at[pl.ds(t * rows, rows), :],
            ))
    started = [
        pltpu.make_async_copy(source, target, sems.at[i])
        for i, (source, target) in enumerate(pairs)
    ]
    for copy in started:
        copy.start()
    if first:
        started[0].wait()
        ids = jnp.broadcast_to(rest[1][...].astype(jnp.float32), (ID_ROWS, rows))
        for out in outs:
            for column in range(0, width, rows):
                out[TENSORS * rows :, column : column + rows] = ids.astype(jnp.bfloat16)
    for copy in started[1 if first else 0 :]:
        copy.wait()


def pack(arrays, slice_ids, gains, groups, local, chunk, width):
    rows = arrays[0].shape[1]
    first = chunk == 0
    height = TENSORS * rows + (ID_ROWS if first else 0)
    vmem_spec = pl.BlockSpec(memory_space=pltpu.VMEM)
    operands = tuple(arrays) + ((slice_ids, *gains) if first else ())
    count = TENSORS * groups + (3 if first else 0)
    gain_shapes = [jax.ShapeDtypeStruct((1, HEAD_DIM), jnp.float32)] * (2 if first else 0)
    outs = pl.pallas_call(
        functools.partial(pack_kernel, groups, local, chunk, width, first),
        out_shape=[jax.ShapeDtypeStruct((height, width), jnp.bfloat16)] * groups + gain_shapes,
        in_specs=[pl.BlockSpec(memory_space=pltpu.HBM)] * len(operands),
        out_specs=[vmem_spec] * (groups + len(gain_shapes)),
        scratch_shapes=[pltpu.SemaphoreType.DMA((count,))]
        + ([pltpu.VMEM((1, rows), jnp.int32)] if first else []),
        compiler_params=pltpu.CompilerParams(vmem_limit_bytes=PACK_MIB * MIB),
        name=f"pack{chunk}",
    )(*operands)
    return outs[:groups], outs[groups:]


def unpack_kernel(groups, local, chunk, width, aliased, *refs):
    pieces, rest = refs[:groups], refs[groups:]
    if aliased:
        rest = rest[TENSORS:]
    outs, sems = rest[:TENSORS], rest[TENSORS]
    rows = outs[0].shape[1]
    started = []
    for shift in range(groups):
        owner = jnp.bitwise_xor(lax.axis_index("seq"), shift)
        start = pl.multiple_of(owner * local + chunk * width, HEAD_DIM)
        for t in range(TENSORS):
            started.append(
                pltpu.make_async_copy(
                    pieces[shift].at[pl.ds(t * rows, rows), :],
                    outs[t].at[0, :, pl.ds(start, width)],
                    sems.at[shift * TENSORS + t],
                )
            )
    for copy in started:
        copy.start()
    for copy in started:
        copy.wait()


def unpack(pieces, previous, shape, local, chunk, width):
    groups = len(pieces)
    aliased = previous is not None
    any_spec = pl.BlockSpec(memory_space=pltpu.HBM)
    vmem_spec = pl.BlockSpec(memory_space=pltpu.VMEM)
    operands = tuple(pieces) + (tuple(previous) if aliased else ())
    aliases = {groups + t: t for t in range(TENSORS)} if aliased else {}
    return pl.pallas_call(
        functools.partial(unpack_kernel, groups, local, chunk, width, aliased),
        out_shape=[jax.ShapeDtypeStruct(shape, jnp.bfloat16)] * TENSORS,
        in_specs=[vmem_spec] * groups + [any_spec] * (len(operands) - groups),
        out_specs=[any_spec] * TENSORS,
        scratch_shapes=[pltpu.SemaphoreType.DMA((groups * TENSORS,))],
        input_output_aliases=aliases,
        compiler_params=pltpu.CompilerParams(vmem_limit_bytes=8 * MIB),
        name=f"unpack{chunk}",
    )(*operands)


def attend_kernel(groups, rows, heads, block, *refs):
    pieces, ids, rest = refs[:groups], refs[groups : 2 * groups], refs[2 * groups :]
    gain_refs, outs, gain_out = rest[:2], rest[2 : 2 + groups], rest[2 + groups]
    length = groups * rows
    query_gain, key_gain = gain_refs[0][...], gain_refs[1][...]
    ids_row = jnp.concatenate([ref[0:1, 0:rows].astype(jnp.float32) for ref in ids], axis=1)
    ids_col = jnp.broadcast_to(ids_row, (HEAD_DIM, length)).T[:, 0:1]
    gain_parts = [jnp.zeros((1, HEAD_DIM), jnp.float32)] * 2
    for head in range(heads):
        cols = slice(head * HEAD_DIM, (head + 1) * HEAD_DIM)

        def gather(t):
            return jnp.concatenate(
                [ref[t * rows : (t + 1) * rows, cols] for ref in pieces], axis=0
            )

        q_normed, q_inv, q_ready = normalize(gather(0), query_gain)
        k_normed, k_inv, k_ready = normalize(gather(1), key_gain)
        values, cotangent = gather(2), gather(3)
        value_acc = key_acc = None
        attended_parts, query_parts = [], []
        for start in range(0, length, block):
            part = slice(start, start + block)
            q_block, grad_block = q_ready[part], cotangent[part]
            scores = dot(q_block, k_ready, (1, 1)) * SCALE
            weights = jnp.where(ids_col[part] == ids_row, jnp.exp(scores), 0.0)
            probs = weights * (1.0 / jnp.sum(weights, axis=1, keepdims=True))
            probs_low = probs.astype(jnp.bfloat16)
            attended = dot(probs_low, values, (1, 0)).astype(jnp.bfloat16)
            row_inner = jnp.sum(
                grad_block.astype(jnp.float32) * attended.astype(jnp.float32),
                axis=1,
                keepdims=True,
            )
            grad_probs = dot(grad_block, values, (1, 1))
            grad_scores = (probs * (grad_probs - row_inner) * SCALE).astype(jnp.bfloat16)
            value_part = dot(probs_low, grad_block, (0, 0))
            key_part = dot(grad_scores, q_block, (0, 0))
            value_acc = value_part if value_acc is None else value_acc + value_part
            key_acc = key_part if key_acc is None else key_acc + key_part
            attended_parts.append(attended)
            query_parts.append(dot(grad_scores, k_ready, (1, 0)))
        attended = jnp.concatenate(attended_parts, axis=0)
        query_acc = jnp.concatenate(query_parts, axis=0)
        query_grad, query_sum = norm_back(query_acc, q_normed, q_inv, query_gain)
        key_grad, key_sum = norm_back(key_acc, k_normed, k_inv, key_gain)
        gain_parts = [gain_parts[0] + query_sum, gain_parts[1] + key_sum]
        results = (attended, query_grad, key_grad, value_acc.astype(jnp.bfloat16))
        for i, out in enumerate(outs):
            for t in range(TENSORS):
                out[t * rows : (t + 1) * rows, cols] = results[t][i * rows : (i + 1) * rows]
    gain_out[0:1, :] = gain_parts[0]
    gain_out[1:2, :] = gain_parts[1]


def attend(pieces, id_holders, query_gain, key_gain, rows, heads, chunk):
    groups = len(pieces)
    width = heads * HEAD_DIM
    length = groups * rows
    height = TENSORS * rows
    block = min(length, 256)
    piece_spec = pl.BlockSpec((height, width), lambda i: (0, 0))
    ids_spec = pl.BlockSpec((ID_ROWS, HEAD_DIM), lambda i: (height // ID_ROWS, 0))
    gain_spec = pl.BlockSpec((1, HEAD_DIM), lambda i: (0, 0))
    area = length * length * heads
    outs = pl.pallas_call(
        functools.partial(attend_kernel, groups, rows, heads, block),
        grid=(1,),
        out_shape=[jax.ShapeDtypeStruct((height, width), jnp.bfloat16)] * groups
        + [jax.ShapeDtypeStruct((2, HEAD_DIM), jnp.float32)],
        in_specs=[piece_spec] * groups + [ids_spec] * groups + [gain_spec] * 2,
        out_specs=[piece_spec] * groups + [pl.BlockSpec((2, HEAD_DIM), lambda i: (0, 0))],
        compiler_params=pltpu.CompilerParams(vmem_limit_bytes=(24 if length <= 512 else 48) * MIB),
        cost_estimate=pl.CostEstimate(
            flops=12 * area * HEAD_DIM,
            bytes_accessed=4 * groups * height * width,
            transcendentals=area,
        ),
        name=f"attend{chunk}",
    )(*pieces, *id_holders, query_gain, key_gain)
    return list(outs[:groups]), outs[groups]


def permute(value, axis, size, shift):
    return lax.ppermute(value, axis, [(i, i ^ shift) for i in range(size)])


def add_parts_kernel(count, *refs):
    parts, out = refs[:count], refs[-1]
    total = parts[0][...]
    for part in parts[1:]:
        total = total + part[...]
    out[...] = total


def add_parts(parts, after):
    vmem_spec = pl.BlockSpec(memory_space=pltpu.VMEM)
    return pl.pallas_call(
        functools.partial(add_parts_kernel, len(parts)),
        out_shape=jax.ShapeDtypeStruct(parts[0].shape, jnp.float32),
        in_specs=[vmem_spec] * len(parts) + [pl.BlockSpec(memory_space=pl.ANY)] * len(after),
        out_specs=vmem_spec,
        compiler_params=pltpu.CompilerParams(vmem_limit_bytes=4 * MIB),
        name="add_parts",
    )(*parts, *after)


def per_device(queries, key_rows, values, cotangent, slice_ids, query_gain, key_gain):
    rows, width = queries.shape[1], queries.shape[2]
    groups, batches = lax.axis_size("seq"), lax.axis_size("dp")
    local = width // groups
    chunks = 2 if local >= 2 * HEAD_DIM else 1
    chunk_width = local // chunks
    heads = chunk_width // HEAD_DIM
    arrays = (queries, key_rows, values, cotangent)
    gains = (query_gain.reshape(1, HEAD_DIM), key_gain.reshape(1, HEAD_DIM))

    received = []
    for chunk in range(chunks):
        payloads, staged = pack(arrays, slice_ids, gains, groups, local, chunk, chunk_width)
        if chunk == 0:
            gains = staged
        received.append(
            [payloads[0]]
            + [permute(payloads[shift], "seq", groups, shift) for shift in range(1, groups)]
        )
    returned, gain_parts = [], []
    for chunk in range(chunks):
        results, gain_part = attend(
            received[chunk], received[0], gains[0], gains[1], rows, heads, chunk
        )
        gain_parts.append(gain_part)
        returned.append(
            [results[0]]
            + [permute(results[shift], "seq", groups, shift) for shift in range(1, groups)]
        )
    gain_total = add_parts(gain_parts, [returned[0][1], returned[0][2]])
    for axis, size in (("dp", batches), ("seq", groups)):
        for step in range(size.bit_length() - 1):
            gain_total = gain_total + permute(gain_total, axis, size, 1 << step)
    outputs = None
    for chunk in range(chunks):
        outputs = unpack(returned[chunk], outputs, queries.shape, local, chunk, chunk_width)
    return (*outputs, gain_total[0], gain_total[1])


def solution(mesh):
    rows = P("dp", "seq", None)
    return jax.shard_map(
        per_device,
        mesh=mesh,
        in_specs=(rows, rows, rows, rows, P("dp", "seq"), P(), P()),
        out_specs=(rows, rows, rows, rows, P(), P()),
        check_vma=False,
    )
```

```python
import functools

import jax
import jax.numpy as jnp
from jax import lax
from jax.experimental import pallas as pl
from jax.experimental.pallas import tpu as pltpu
from jax.sharding import PartitionSpec as P

HEAD_DIM = 128
EPS = 1e-06
TENSORS = 4
ID_ROWS = 16
SCALE = HEAD_DIM ** (-0.5)
MIB = 1024 * 1024


def dot(a, b, contract):
    return lax.dot_general(
        a, b, ((contract[:1], contract[1:]), ((), ())), preferred_element_type=jnp.float32
    )


def normalize(rows, gain):
    floats = rows.astype(jnp.float32)
    inv_rms = lax.rsqrt(jnp.mean(floats * floats, axis=-1, keepdims=True) + EPS)
    normed = floats * inv_rms
    return normed, inv_rms, (normed * gain).astype(jnp.bfloat16)


def norm_back(grad_out, normed, inv_rms, gain):
    grad_normed = grad_out * gain
    inner_mean = jnp.mean(grad_normed * normed, axis=-1, keepdims=True)
    grad_rows = (inv_rms * (grad_normed - normed * inner_mean)).astype(jnp.bfloat16)
    return grad_rows, jnp.sum(grad_out * normed, axis=0, keepdims=True)


def pack_kernel(groups, local, chunk, width, first, *refs):
    tensors, rest = refs[:TENSORS], refs[TENSORS:]
    if first:
        (ids_ref, *gain_refs), rest = rest[:3], rest[3:]
    outs, rest = rest[:groups], rest[groups:]
    if first:
        gain_outs, rest = rest[:2], rest[2:]
    sems = rest[0]
    rows = tensors[0].shape[1]
    pairs = []
    if first:
        pairs.append((ids_ref, rest[1]))
        pairs.extend(zip(gain_refs, gain_outs))
    for shift in range(groups):
        owner = jnp.bitwise_xor(lax.axis_index("seq"), shift)
        start = pl.multiple_of(owner * local + chunk * width, HEAD_DIM)
        for t in range(TENSORS):
            pairs.append((
                tensors[t].at[0, :, pl.ds(start, width)],
                outs[shift].at[pl.ds(t * rows, rows), :],
            ))
    started = [
        pltpu.make_async_copy(source, target, sems.at[i])
        for i, (source, target) in enumerate(pairs)
    ]
    for copy in started:
        copy.start()
    if first:
        started[0].wait()
        ids = jnp.broadcast_to(rest[1][...].astype(jnp.float32), (ID_ROWS, rows))
        for out in outs:
            for column in range(0, width, rows):
                out[TENSORS * rows :, column : column + rows] = ids.astype(jnp.bfloat16)
    for copy in started[1 if first else 0 :]:
        copy.wait()


def pack(arrays, slice_ids, gains, groups, local, chunk, width):
    rows = arrays[0].shape[1]
    first = chunk == 0
    height = TENSORS * rows + (ID_ROWS if first else 0)
    vmem_spec = pl.BlockSpec(memory_space=pltpu.VMEM)
    operands = tuple(
        pltpu.with_memory_space_constraint(x, pltpu.HBM)
        for x in tuple(arrays) + ((slice_ids, *gains) if first else ())
    )
    count = TENSORS * groups + (3 if first else 0)
    gain_shapes = [jax.ShapeDtypeStruct((1, HEAD_DIM), jnp.float32)] * (2 if first else 0)
    outs = pl.pallas_call(
        functools.partial(pack_kernel, groups, local, chunk, width, first),
        out_shape=[jax.ShapeDtypeStruct((height, width), jnp.bfloat16)] * groups + gain_shapes,
        in_specs=[pl.BlockSpec(memory_space=pltpu.HBM)] * len(operands),
        out_specs=[vmem_spec] * (groups + len(gain_shapes)),
        scratch_shapes=[pltpu.SemaphoreType.DMA((count,))]
        + ([pltpu.VMEM((1, rows), jnp.int32)] if first else []),
        compiler_params=pltpu.CompilerParams(vmem_limit_bytes=8 * MIB),
        name=f"pack{chunk}",
    )(*operands)
    return outs[:groups], outs[groups:]


def unpack_kernel(groups, local, chunk, width, aliased, *refs):
    pieces, rest = refs[:groups], refs[groups:]
    if aliased:
        rest = rest[TENSORS:]
    outs, sems = rest[:TENSORS], rest[TENSORS]
    rows = outs[0].shape[1]
    started = []
    for shift in range(groups):
        owner = jnp.bitwise_xor(lax.axis_index("seq"), shift)
        start = pl.multiple_of(owner * local + chunk * width, HEAD_DIM)
        for t in range(TENSORS):
            started.append(
                pltpu.make_async_copy(
                    pieces[shift].at[pl.ds(t * rows, rows), :],
                    outs[t].at[0, :, pl.ds(start, width)],
                    sems.at[shift * TENSORS + t],
                )
            )
    for copy in started:
        copy.start()
    for copy in started:
        copy.wait()


def unpack(pieces, previous, shape, local, chunk, width):
    groups = len(pieces)
    aliased = previous is not None
    any_spec = pl.BlockSpec(memory_space=pltpu.HBM)
    vmem_spec = pl.BlockSpec(memory_space=pltpu.VMEM)
    operands = tuple(pieces) + (tuple(previous) if aliased else ())
    aliases = {groups + t: t for t in range(TENSORS)} if aliased else {}
    return pl.pallas_call(
        functools.partial(unpack_kernel, groups, local, chunk, width, aliased),
        out_shape=[jax.ShapeDtypeStruct(shape, jnp.bfloat16)] * TENSORS,
        in_specs=[vmem_spec] * groups + [any_spec] * (len(operands) - groups),
        out_specs=[any_spec] * TENSORS,
        scratch_shapes=[pltpu.SemaphoreType.DMA((groups * TENSORS,))],
        input_output_aliases=aliases,
        compiler_params=pltpu.CompilerParams(vmem_limit_bytes=8 * MIB),
        name=f"unpack{chunk}",
    )(*operands)


def attend_kernel(groups, rows, heads, block, *refs):
    pieces, ids, rest = refs[:groups], refs[groups : 2 * groups], refs[2 * groups :]
    gain_refs, outs, gain_out = rest[:2], rest[2 : 2 + groups], rest[2 + groups]
    length = groups * rows
    query_gain, key_gain = gain_refs[0][...], gain_refs[1][...]
    ids_row = jnp.concatenate([ref[0:1, 0:rows].astype(jnp.float32) for ref in ids], axis=1)
    ids_col = jnp.broadcast_to(ids_row, (HEAD_DIM, length)).T[:, 0:1]
    gain_parts = [jnp.zeros((1, HEAD_DIM), jnp.float32)] * 2
    for head in range(heads):
        cols = slice(head * HEAD_DIM, (head + 1) * HEAD_DIM)

        def gather(t):
            return jnp.concatenate(
                [ref[t * rows : (t + 1) * rows, cols] for ref in pieces], axis=0
            )

        q_normed, q_inv, q_ready = normalize(gather(0), query_gain)
        k_normed, k_inv, k_ready = normalize(gather(1), key_gain)
        values, cotangent = gather(2), gather(3)
        value_acc = key_acc = None
        attended_parts, query_parts = [], []
        for start in range(0, length, block):
            part = slice(start, start + block)
            q_block, grad_block = q_ready[part], cotangent[part]
            scores = dot(q_block, k_ready, (1, 1)) * SCALE
            weights = jnp.where(ids_col[part] == ids_row, jnp.exp(scores), 0.0)
            probs = weights * (1.0 / jnp.sum(weights, axis=1, keepdims=True))
            probs_low = probs.astype(jnp.bfloat16)
            attended = dot(probs_low, values, (1, 0)).astype(jnp.bfloat16)
            row_inner = jnp.sum(
                grad_block.astype(jnp.float32) * attended.astype(jnp.float32),
                axis=1,
                keepdims=True,
            )
            grad_probs = dot(grad_block, values, (1, 1))
            grad_scores = (probs * (grad_probs - row_inner) * SCALE).astype(jnp.bfloat16)
            value_part = dot(probs_low, grad_block, (0, 0))
            key_part = dot(grad_scores, q_block, (0, 0))
            value_acc = value_part if value_acc is None else value_acc + value_part
            key_acc = key_part if key_acc is None else key_acc + key_part
            attended_parts.append(attended)
            query_parts.append(dot(grad_scores, k_ready, (1, 0)))
        attended = jnp.concatenate(attended_parts, axis=0)
        query_acc = jnp.concatenate(query_parts, axis=0)
        query_grad, query_sum = norm_back(query_acc, q_normed, q_inv, query_gain)
        key_grad, key_sum = norm_back(key_acc, k_normed, k_inv, key_gain)
        gain_parts = [gain_parts[0] + query_sum, gain_parts[1] + key_sum]
        results = (attended, query_grad, key_grad, value_acc.astype(jnp.bfloat16))
        for i, out in enumerate(outs):
            for t in range(TENSORS):
                out[t * rows : (t + 1) * rows, cols] = results[t][i * rows : (i + 1) * rows]
    gain_out[0:1, :] = gain_parts[0]
    gain_out[1:2, :] = gain_parts[1]


def attend(pieces, id_holders, query_gain, key_gain, rows, heads, chunk):
    groups = len(pieces)
    width = heads * HEAD_DIM
    length = groups * rows
    height = TENSORS * rows
    block = min(length, 256)
    piece_spec = pl.BlockSpec((height, width), lambda i: (0, 0))
    ids_spec = pl.BlockSpec((ID_ROWS, HEAD_DIM), lambda i: (height // ID_ROWS, 0))
    gain_spec = pl.BlockSpec((1, HEAD_DIM), lambda i: (0, 0))
    area = length * length * heads
    outs = pl.pallas_call(
        functools.partial(attend_kernel, groups, rows, heads, block),
        grid=(1,),
        out_shape=[jax.ShapeDtypeStruct((height, width), jnp.bfloat16)] * groups
        + [jax.ShapeDtypeStruct((2, HEAD_DIM), jnp.float32)],
        in_specs=[piece_spec] * groups + [ids_spec] * groups + [gain_spec] * 2,
        out_specs=[piece_spec] * groups + [pl.BlockSpec((2, HEAD_DIM), lambda i: (0, 0))],
        compiler_params=pltpu.CompilerParams(vmem_limit_bytes=(24 if length <= 512 else 48) * MIB),
        cost_estimate=pl.CostEstimate(
            flops=12 * area * HEAD_DIM,
            bytes_accessed=4 * groups * height * width,
            transcendentals=area,
        ),
        name=f"attend{chunk}",
    )(*pieces, *id_holders, query_gain, key_gain)
    return list(outs[:groups]), outs[groups]


def permute(value, axis, size, shift):
    return lax.ppermute(value, axis, [(i, i ^ shift) for i in range(size)])


def add_parts_kernel(count, *refs):
    parts, out = refs[:count], refs[-1]
    total = parts[0][...]
    for part in parts[1:]:
        total = total + part[...]
    out[...] = jnp.broadcast_to(total[None], out.shape)


def add_parts(parts, after, copies):
    vmem_spec = pl.BlockSpec(memory_space=pltpu.VMEM)
    return pl.pallas_call(
        functools.partial(add_parts_kernel, len(parts)),
        out_shape=jax.ShapeDtypeStruct((copies, *parts[0].shape), jnp.float32),
        in_specs=[vmem_spec] * len(parts) + [pl.BlockSpec(memory_space=pl.ANY)] * len(after),
        out_specs=vmem_spec,
        compiler_params=pltpu.CompilerParams(vmem_limit_bytes=4 * MIB),
        name="add_parts",
    )(*parts, *after)


def per_device(queries, key_rows, values, cotangent, slice_ids, query_gain, key_gain):
    rows, width = queries.shape[1], queries.shape[2]
    groups, batches = lax.axis_size("seq"), lax.axis_size("dp")
    local = width // groups
    chunks = 2 if local >= 2 * HEAD_DIM else 1
    chunk_width = local // chunks
    heads = chunk_width // HEAD_DIM
    arrays = (queries, key_rows, values, cotangent)
    gains = (query_gain.reshape(1, HEAD_DIM), key_gain.reshape(1, HEAD_DIM))

    received = []
    for chunk in range(chunks):
        payloads, staged = pack(arrays, slice_ids, gains, groups, local, chunk, chunk_width)
        if chunk == 0:
            gains = staged
        received.append(
            [payloads[0]]
            + [permute(payloads[shift], "seq", groups, shift) for shift in range(1, groups)]
        )
    returned, gain_parts = [], []
    for chunk in range(chunks):
        results, gain_part = attend(
            received[chunk], received[0], gains[0], gains[1], rows, heads, chunk
        )
        gain_parts.append(gain_part)
        returned.append(
            [results[0]]
            + [permute(results[shift], "seq", groups, shift) for shift in range(1, groups)]
        )
    copies = add_parts(gain_parts, [returned[0][1], returned[0][2]], batches * groups)
    gain_total = lax.all_to_all(
        copies, ("dp", "seq"), split_axis=0, concat_axis=0, tiled=True
    ).sum(0)
    outputs = None
    for chunk in range(chunks):
        outputs = unpack(returned[chunk], outputs, queries.shape, local, chunk, chunk_width)
    return (*outputs, gain_total[0], gain_total[1])


def solution(mesh):
    rows = P("dp", "seq", None)
    return jax.shard_map(
        per_device,
        mesh=mesh,
        in_specs=(rows, rows, rows, rows, P("dp", "seq"), P(), P()),
        out_specs=(rows, rows, rows, rows, P(), P()),
        check_vma=False,
    )
```

```python
import functools

import jax
import jax.numpy as jnp
from jax import lax
from jax.experimental import pallas as pl
from jax.experimental.pallas import tpu as pltpu
from jax.sharding import PartitionSpec as P

HEAD_DIM = 128
EPS = 1e-06
TENSORS = 4
ID_ROWS = 16
LOG2_E = 1.4426950408889634
SCALE = HEAD_DIM ** (-0.5)
MIB = 1024 * 1024


def dot(a, b, contract):
    return lax.dot_general(
        a, b, ((contract[:1], contract[1:]), ((), ())), preferred_element_type=jnp.float32
    )


def normalize(rows, gain):
    floats = rows.astype(jnp.float32)
    inv_rms = lax.rsqrt(jnp.mean(floats * floats, axis=-1, keepdims=True) + EPS)
    normed = floats * inv_rms
    return normed, inv_rms, (normed * gain).astype(jnp.bfloat16)


def norm_back(grad_out, normed, inv_rms, gain):
    grad_normed = grad_out * gain
    inner_mean = jnp.mean(grad_normed * normed, axis=-1, keepdims=True)
    grad_rows = (inv_rms * (grad_normed - normed * inner_mean)).astype(jnp.bfloat16)
    return grad_rows, jnp.sum(grad_out * normed, axis=0, keepdims=True)


def pack_kernel(shifts, local, chunk, width, with_ids, gain_count, *refs):
    tensors, rest = refs[:TENSORS], refs[TENSORS:]
    if with_ids:
        ids_ref, rest = rest[0], rest[1:]
    gain_refs, rest = rest[:gain_count], rest[gain_count:]
    outs, rest = rest[: len(shifts)], rest[len(shifts) :]
    gain_outs, rest = rest[:gain_count], rest[gain_count:]
    sems = rest[0]
    rows = tensors[0].shape[1]
    pairs = [(ids_ref, rest[1])] if with_ids else []
    for out, shift in zip(outs, shifts):
        owner = jnp.bitwise_xor(lax.axis_index("seq"), shift)
        start = pl.multiple_of(owner * local + chunk * width, HEAD_DIM)
        for t in range(TENSORS):
            pairs.append((
                tensors[t].at[0, :, pl.ds(start, width)],
                out.at[pl.ds(t * rows, rows), :],
            ))
    pairs.extend(zip(gain_refs, gain_outs))
    started = [
        pltpu.make_async_copy(source, target, sems.at[i])
        for i, (source, target) in enumerate(pairs)
    ]
    for copy in started:
        copy.start()
    if with_ids:
        started[0].wait()
        ids = jnp.broadcast_to(rest[1][...].astype(jnp.float32), (ID_ROWS, rows))
        for out in outs:
            for column in range(0, width, rows):
                out[TENSORS * rows :, column : column + rows] = ids.astype(jnp.bfloat16)
    for copy in started[1 if with_ids else 0 :]:
        copy.wait()


def pack(arrays, slice_ids, gains, shifts, local, chunk, width, label):
    rows = arrays[0].shape[1]
    with_ids = slice_ids is not None
    height = TENSORS * rows + (ID_ROWS if with_ids else 0)
    vmem_spec = pl.BlockSpec(memory_space=pltpu.VMEM)
    operands = tuple(
        pltpu.with_memory_space_constraint(x, pltpu.HBM)
        for x in (*arrays, *([slice_ids] if with_ids else []), *gains)
    )
    count = TENSORS * len(shifts) + len(gains) + (1 if with_ids else 0)
    outs = pl.pallas_call(
        functools.partial(
            pack_kernel, tuple(shifts), local, chunk, width, with_ids, len(gains)
        ),
        out_shape=[jax.ShapeDtypeStruct((height, width), jnp.bfloat16)] * len(shifts)
        + [jax.ShapeDtypeStruct((1, HEAD_DIM), jnp.float32)] * len(gains),
        in_specs=[pl.BlockSpec(memory_space=pltpu.HBM)] * len(operands),
        out_specs=[vmem_spec] * (len(shifts) + len(gains)),
        scratch_shapes=[pltpu.SemaphoreType.DMA((count,))]
        + ([pltpu.VMEM((1, rows), jnp.int32)] if with_ids else []),
        compiler_params=pltpu.CompilerParams(vmem_limit_bytes=8 * MIB),
        name=label,
    )(*operands)
    return dict(zip(shifts, outs)), outs[len(shifts) :]


def unpack_kernel(places, count, local, width, aliased, with_gains, *refs):
    pieces, rest = refs[:count], refs[count:]
    if with_gains:
        gain_ref, rest = rest[0], rest[1:]
    if aliased:
        rest = rest[TENSORS:]
    outs, rest = rest[:TENSORS], rest[TENSORS:]
    if with_gains:
        gain_outs, totals, rest = rest[:2], rest[2], rest[3:]
    sems = rest[0]
    rows = outs[0].shape[1]
    started = []
    for operand, shift, chunk in places:
        owner = jnp.bitwise_xor(lax.axis_index("seq"), shift)
        start = pl.multiple_of(owner * local + chunk * width, HEAD_DIM)
        for t in range(TENSORS):
            started.append(
                pltpu.make_async_copy(
                    pieces[operand].at[pl.ds(t * rows, rows), :],
                    outs[t].at[0, :, pl.ds(start, width)],
                    sems.at[len(started)],
                )
            )
    for copy in started:
        copy.start()
    if with_gains:
        totals[...] = jnp.sum(gain_ref[...], axis=0)
        for i, out in enumerate(gain_outs):
            started.append(
                pltpu.make_async_copy(totals.at[i], out.at[0], sems.at[len(started)])
            )
            started[-1].start()
    for copy in started:
        copy.wait()


def unpack(entries, gain_sums, previous, shape, local, width, label):
    pieces = [piece for piece, _, _ in entries]
    places = [(i, shift, chunk) for i, (_, shift, chunk) in enumerate(entries)]
    count, aliased, with_gains = len(pieces), previous is not None, gain_sums is not None
    hbm_spec = pl.BlockSpec(memory_space=pltpu.HBM)
    vmem_spec = pl.BlockSpec(memory_space=pltpu.VMEM)
    read = (*pieces, *([gain_sums] if with_gains else []))
    operands = (*read, *(previous if aliased else ()))
    gain_outs = 2 if with_gains else 0
    return pl.pallas_call(
        functools.partial(unpack_kernel, places, count, local, width, aliased, with_gains),
        out_shape=[jax.ShapeDtypeStruct(shape, jnp.bfloat16)] * TENSORS
        + [jax.ShapeDtypeStruct((1, HEAD_DIM), jnp.float32)] * gain_outs,
        in_specs=[vmem_spec] * len(read) + [hbm_spec] * (len(operands) - len(read)),
        out_specs=[hbm_spec] * (TENSORS + gain_outs),
        scratch_shapes=[pltpu.VMEM((2, HEAD_DIM), jnp.float32)] * (1 if with_gains else 0)
        + [pltpu.SemaphoreType.DMA((count * TENSORS + gain_outs,))],
        input_output_aliases={len(read) + t: t for t in range(TENSORS)} if aliased else {},
        compiler_params=pltpu.CompilerParams(vmem_limit_bytes=8 * MIB),
        name=label,
    )(*operands)


def attend_kernel(groups, rows, heads, block, *refs):
    pieces, ids, rest = refs[:groups], refs[groups : 2 * groups], refs[2 * groups :]
    gain_refs, outs, gain_out = rest[:2], rest[2 : 2 + groups], rest[2 + groups]
    length = groups * rows
    query_gain, key_gain = gain_refs[0][...], gain_refs[1][...]
    ids_row = jnp.concatenate([ref[0:1, 0:rows].astype(jnp.float32) for ref in ids], axis=1)
    ids_col = jnp.broadcast_to(ids_row, (HEAD_DIM, length)).T
    lane = lax.broadcasted_iota(jnp.int32, (length, HEAD_DIM), 1)
    of_slice = jnp.where(lane == 0, ids_col, jnp.where(lane == 1, 1.0 - ids_col, 0.0))
    not_slice = jnp.where(lane == 0, 1.0 - ids_col, jnp.where(lane == 1, ids_col, 0.0))
    q_marks = (64.0 * of_slice).astype(jnp.bfloat16)
    k_marks = (-64.0 * not_slice).astype(jnp.bfloat16)
    gain_parts = [jnp.zeros((1, HEAD_DIM), jnp.float32)] * 2
    for head in range(heads):
        cols = slice(head * HEAD_DIM, (head + 1) * HEAD_DIM)

        def gather(t):
            return jnp.concatenate(
                [ref[t * rows : (t + 1) * rows, cols] for ref in pieces], axis=0
            )

        q_normed, q_inv, q_ready = normalize(gather(0), query_gain)
        k_normed, k_inv, k_ready = normalize(gather(1), key_gain)
        values, cotangent = gather(2), gather(3)
        k_marked = jnp.concatenate([k_ready, k_marks], axis=1)
        value_acc = key_acc = None
        attended_parts, query_parts = [], []
        for start in range(0, length, block):
            part = slice(start, start + block)
            q_block, grad_block = q_ready[part], cotangent[part]
            scores = dot(jnp.concatenate([q_block, q_marks[part]], axis=1), k_marked, (1, 1)) * (SCALE * LOG2_E)
            weights = jnp.exp2(scores)
            probs = weights * (1.0 / jnp.sum(weights, axis=1, keepdims=True))
            probs_low = probs.astype(jnp.bfloat16)
            attended = dot(probs_low, values, (1, 0)).astype(jnp.bfloat16)
            row_inner = jnp.sum(
                grad_block.astype(jnp.float32) * attended.astype(jnp.float32),
                axis=1,
                keepdims=True,
            )
            grad_probs = dot(grad_block, values, (1, 1))
            grad_scores = (probs * (grad_probs - row_inner)).astype(jnp.bfloat16)
            value_part = dot(grad_block, probs_low, (0, 0))
            key_part = dot(q_block, grad_scores, (0, 0))
            value_acc = value_part if value_acc is None else value_acc + value_part
            key_acc = key_part if key_acc is None else key_acc + key_part
            attended_parts.append(attended)
            query_parts.append(dot(grad_scores, k_ready, (1, 0)))
        value_acc, key_acc = value_acc.T, key_acc.T
        attended = jnp.concatenate(attended_parts, axis=0)
        query_acc = jnp.concatenate(query_parts, axis=0) * SCALE
        query_grad, query_sum = norm_back(query_acc, q_normed, q_inv, query_gain)
        key_grad, key_sum = norm_back(key_acc * SCALE, k_normed, k_inv, key_gain)
        gain_parts = [gain_parts[0] + query_sum, gain_parts[1] + key_sum]
        results = (attended, query_grad, key_grad, value_acc.astype(jnp.bfloat16))
        for i, out in enumerate(outs):
            for t in range(TENSORS):
                out[t * rows : (t + 1) * rows, cols] = results[t][i * rows : (i + 1) * rows]
    gain_out[0:1, :] = gain_parts[0]
    gain_out[1:2, :] = gain_parts[1]


def attend(pieces, id_holders, query_gain, key_gain, rows, heads, chunk):
    groups = len(pieces)
    width = heads * HEAD_DIM
    length = groups * rows
    height = TENSORS * rows
    block = min(length, 512 if length <= 512 else 256)
    piece_spec = pl.BlockSpec((height, width), lambda i: (0, 0))
    ids_spec = pl.BlockSpec((ID_ROWS, HEAD_DIM), lambda i: (height // ID_ROWS, 0))
    gain_spec = pl.BlockSpec((1, HEAD_DIM), lambda i: (0, 0))
    area = length * length * heads
    outs = pl.pallas_call(
        functools.partial(attend_kernel, groups, rows, heads, block),
        grid=(1,),
        out_shape=[jax.ShapeDtypeStruct((height, width), jnp.bfloat16)] * groups
        + [jax.ShapeDtypeStruct((2, HEAD_DIM), jnp.float32)],
        in_specs=[piece_spec] * groups + [ids_spec] * groups + [gain_spec] * 2,
        out_specs=[piece_spec] * groups + [pl.BlockSpec((2, HEAD_DIM), lambda i: (0, 0))],
        compiler_params=pltpu.CompilerParams(vmem_limit_bytes=(24 if length <= 512 else 48) * MIB),
        cost_estimate=pl.CostEstimate(
            flops=12 * area * HEAD_DIM,
            bytes_accessed=4 * groups * height * width,
            transcendentals=area,
        ),
        name=f"attend{chunk}",
    )(*pieces, *id_holders, query_gain, key_gain)
    return list(outs[:groups]), outs[groups]


def permute(value, axis, size, shift):
    return lax.ppermute(value, axis, [(i, i ^ shift) for i in range(size)])


def add_parts_kernel(*refs):
    *parts, out = refs
    total = parts[0][...]
    for part in parts[1:]:
        total = total + part[...]
    out[...] = jnp.broadcast_to(total[None], out.shape)


def add_parts(parts, copies):
    vmem_spec = pl.BlockSpec(memory_space=pltpu.VMEM)
    return pl.pallas_call(
        add_parts_kernel,
        out_shape=jax.ShapeDtypeStruct((copies, *parts[0].shape), jnp.float32),
        in_specs=[vmem_spec] * len(parts),
        out_specs=vmem_spec,
        compiler_params=pltpu.CompilerParams(vmem_limit_bytes=4 * MIB),
        name="add_parts",
    )(*parts)


def per_device(queries, key_rows, values, cotangent, slice_ids, query_gain, key_gain):
    rows, width = queries.shape[1], queries.shape[2]
    groups, batches = lax.axis_size("seq"), lax.axis_size("dp")
    local = width // groups
    chunks = 2 if local >= 2 * HEAD_DIM else 1
    chunk_width = local // chunks
    heads = chunk_width // HEAD_DIM
    arrays = (queries, key_rows, values, cotangent)
    gains = (query_gain.reshape(1, HEAD_DIM), key_gain.reshape(1, HEAD_DIM))

    peers = list(range(1, groups))
    every = list(range(chunks))
    received = []
    for chunk in every:
        if chunk == 0:
            payloads, _ = pack(
                arrays, slice_ids, (), peers[-1:], local, chunk, chunk_width, "pack_far"
            )
            rest, gains = pack(
                arrays, slice_ids, gains, peers[:-1] + [0], local, chunk, chunk_width, "pack"
            )
            payloads.update(rest)
        else:
            payloads, _ = pack(
                arrays, None, (), peers + [0], local, chunk, chunk_width, "pack_next"
            )
        received.append(
            [payloads[0]] + [permute(payloads[shift], "seq", groups, shift) for shift in peers]
        )
    returned, gain_parts = [], []
    for chunk in range(chunks):
        results, gain_part = attend(
            received[chunk], received[0], gains[0], gains[1], rows, heads, chunk
        )
        gain_parts.append(gain_part)
        returned.append(
            [results[0]] + [permute(results[shift], "seq", groups, shift) for shift in peers]
        )
    gain_sums = lax.all_to_all(
        add_parts(gain_parts, batches * groups),
        ("dp", "seq"),
        split_axis=0,
        concat_axis=0,
        tiled=True,
    )
    early = [(returned[chunk][0], 0, chunk) for chunk in every]
    early += [(returned[chunk][s], s, chunk) for chunk in every[:-1] for s in peers]
    late = [(returned[-1][s], s, chunks - 1) for s in peers]
    outputs = unpack(early, None, None, queries.shape, local, chunk_width, "unpack")
    *outputs, query_total, key_total = unpack(
        late, gain_sums, outputs, queries.shape, local, chunk_width, "unpack_last"
    )
    return (*outputs, query_total.reshape(HEAD_DIM), key_total.reshape(HEAD_DIM))


def solution(mesh):
    rows = P("dp", "seq", None)
    return jax.shard_map(
        per_device,
        mesh=mesh,
        in_specs=(rows, rows, rows, rows, P("dp", "seq"), P(), P()),
        out_specs=(rows, rows, rows, rows, P(), P()),
        check_vma=False,
    )
```

```python
import functools

import jax
import jax.numpy as jnp
from jax import lax
from jax.experimental import pallas as pl
from jax.experimental.pallas import tpu as pltpu
from jax.sharding import PartitionSpec as P

HEAD_DIM = 128
EPS = 1e-06
TENSORS = 4
ID_ROWS = 16
LOG2_E = 1.4426950408889634
SCALE = HEAD_DIM ** (-0.5)
MIB = 1024 * 1024


def dot(a, b, contract):
    return lax.dot_general(
        a, b, ((contract[:1], contract[1:]), ((), ())), preferred_element_type=jnp.float32
    )


def normalize(rows, gain):
    floats = rows.astype(jnp.float32)
    inv_rms = lax.rsqrt(jnp.mean(floats * floats, axis=-1, keepdims=True) + EPS)
    normed = floats * inv_rms
    return normed, inv_rms, (normed * gain).astype(jnp.bfloat16)


def norm_back(grad_out, normed, inv_rms, gain):
    grad_normed = grad_out * gain
    inner_mean = jnp.mean(grad_normed * normed, axis=-1, keepdims=True)
    grad_rows = (inv_rms * (grad_normed - normed * inner_mean)).astype(jnp.bfloat16)
    return grad_rows, jnp.sum(grad_out * normed, axis=0, keepdims=True)


def pack_kernel(shifts, local, chunk, width, with_ids, gain_count, *refs):
    tensors, rest = refs[:TENSORS], refs[TENSORS:]
    if with_ids:
        ids_ref, rest = rest[0], rest[1:]
    gain_refs, rest = rest[:gain_count], rest[gain_count:]
    outs, rest = rest[: len(shifts)], rest[len(shifts) :]
    gain_outs, rest = rest[:gain_count], rest[gain_count:]
    sems = rest[0]
    rows = tensors[0].shape[1]
    pairs = [(ids_ref, rest[1])] if with_ids else []
    for out, shift in zip(outs, shifts):
        owner = jnp.bitwise_xor(lax.axis_index("seq"), shift)
        start = pl.multiple_of(owner * local + chunk * width, HEAD_DIM)
        for t in range(TENSORS):
            pairs.append((
                tensors[t].at[0, :, pl.ds(start, width)],
                out.at[pl.ds(t * rows, rows), :],
            ))
    pairs.extend(zip(gain_refs, gain_outs))
    started = [
        pltpu.make_async_copy(source, target, sems.at[i])
        for i, (source, target) in enumerate(pairs)
    ]
    for copy in started:
        copy.start()
    if with_ids:
        started[0].wait()
        ids = jnp.broadcast_to(rest[1][...].astype(jnp.float32), (ID_ROWS, rows))
        for out in outs:
            for column in range(0, width, rows):
                out[TENSORS * rows :, column : column + rows] = ids.astype(jnp.bfloat16)
    for copy in started[1 if with_ids else 0 :]:
        copy.wait()


def pack(arrays, slice_ids, gains, shifts, local, chunk, width, label):
    rows = arrays[0].shape[1]
    with_ids = slice_ids is not None
    height = TENSORS * rows + (ID_ROWS if with_ids else 0)
    vmem_spec = pl.BlockSpec(memory_space=pltpu.VMEM)
    operands = tuple(
        pltpu.with_memory_space_constraint(x, pltpu.HBM)
        for x in (*arrays, *([slice_ids] if with_ids else []), *gains)
    )
    count = TENSORS * len(shifts) + len(gains) + (1 if with_ids else 0)
    outs = pl.pallas_call(
        functools.partial(
            pack_kernel, tuple(shifts), local, chunk, width, with_ids, len(gains)
        ),
        out_shape=[jax.ShapeDtypeStruct((height, width), jnp.bfloat16)] * len(shifts)
        + [jax.ShapeDtypeStruct((1, HEAD_DIM), jnp.float32)] * len(gains),
        in_specs=[pl.BlockSpec(memory_space=pltpu.HBM)] * len(operands),
        out_specs=[vmem_spec] * (len(shifts) + len(gains)),
        scratch_shapes=[pltpu.SemaphoreType.DMA((count,))]
        + ([pltpu.VMEM((1, rows), jnp.int32)] if with_ids else []),
        compiler_params=pltpu.CompilerParams(vmem_limit_bytes=8 * MIB),
        name=label,
    )(*operands)
    return dict(zip(shifts, outs)), outs[len(shifts) :]


def unpack_kernel(places, count, local, width, aliased, with_gains, *refs):
    pieces, rest = refs[:count], refs[count:]
    if with_gains:
        gain_ref, rest = rest[0], rest[1:]
    if aliased:
        rest = rest[TENSORS:]
    outs, rest = rest[:TENSORS], rest[TENSORS:]
    if with_gains:
        gain_outs, totals, rest = rest[:2], rest[2], rest[3:]
    sems = rest[0]
    rows = outs[0].shape[1]
    started = []
    for operand, shift, chunk in places:
        owner = jnp.bitwise_xor(lax.axis_index("seq"), shift)
        start = pl.multiple_of(owner * local + chunk * width, HEAD_DIM)
        for t in range(TENSORS):
            started.append(
                pltpu.make_async_copy(
                    pieces[operand].at[pl.ds(t * rows, rows), :],
                    outs[t].at[0, :, pl.ds(start, width)],
                    sems.at[len(started)],
                )
            )
    for copy in started:
        copy.start()
    if with_gains:
        totals[...] = jnp.sum(gain_ref[...], axis=0)
        for i, out in enumerate(gain_outs):
            started.append(
                pltpu.make_async_copy(totals.at[i], out.at[0], sems.at[len(started)])
            )
            started[-1].start()
    for copy in started:
        copy.wait()


def unpack(entries, gain_sums, previous, shape, local, width, label):
    pieces = [piece for piece, _, _ in entries]
    places = [(i, shift, chunk) for i, (_, shift, chunk) in enumerate(entries)]
    count, aliased, with_gains = len(pieces), previous is not None, gain_sums is not None
    hbm_spec = pl.BlockSpec(memory_space=pltpu.HBM)
    vmem_spec = pl.BlockSpec(memory_space=pltpu.VMEM)
    read = (*pieces, *([gain_sums] if with_gains else []))
    operands = (*read, *(previous if aliased else ()))
    gain_outs = 2 if with_gains else 0
    return pl.pallas_call(
        functools.partial(unpack_kernel, places, count, local, width, aliased, with_gains),
        out_shape=[jax.ShapeDtypeStruct(shape, jnp.bfloat16)] * TENSORS
        + [jax.ShapeDtypeStruct((1, HEAD_DIM), jnp.float32)] * gain_outs,
        in_specs=[vmem_spec] * len(read) + [hbm_spec] * (len(operands) - len(read)),
        out_specs=[hbm_spec] * (TENSORS + gain_outs),
        scratch_shapes=[pltpu.VMEM((2, HEAD_DIM), jnp.float32)] * (1 if with_gains else 0)
        + [pltpu.SemaphoreType.DMA((count * TENSORS + gain_outs,))],
        input_output_aliases={len(read) + t: t for t in range(TENSORS)} if aliased else {},
        compiler_params=pltpu.CompilerParams(vmem_limit_bytes=8 * MIB),
        name=label,
    )(*operands)


def attend_kernel(groups, rows, heads, block, *refs):
    pieces, ids, rest = refs[:groups], refs[groups : 2 * groups], refs[2 * groups :]
    gain_refs, outs, gain_out = rest[:2], rest[2 : 2 + groups], rest[2 + groups]
    length = groups * rows
    query_gain, key_gain = gain_refs[0][...], gain_refs[1][...]
    ids_row = jnp.concatenate([ref[0:1, 0:rows].astype(jnp.float32) for ref in ids], axis=1)
    ids_col = jnp.broadcast_to(ids_row, (HEAD_DIM, length)).T
    lane = lax.broadcasted_iota(jnp.int32, (length, HEAD_DIM), 1)
    of_slice = jnp.where(lane == 0, ids_col, jnp.where(lane == 1, 1.0 - ids_col, 0.0))
    not_slice = jnp.where(lane == 0, 1.0 - ids_col, jnp.where(lane == 1, ids_col, 0.0))
    q_marks = (64.0 * of_slice).astype(jnp.bfloat16)
    k_marks = (-64.0 * not_slice).astype(jnp.bfloat16)
    gain_parts = [jnp.zeros((1, HEAD_DIM), jnp.float32)] * 2
    for head in range(heads):
        cols = slice(head * HEAD_DIM, (head + 1) * HEAD_DIM)

        def gather(t):
            return jnp.concatenate(
                [ref[t * rows : (t + 1) * rows, cols] for ref in pieces], axis=0
            )

        q_normed, q_inv, q_ready = normalize(gather(0), query_gain)
        k_normed, k_inv, k_ready = normalize(gather(1), key_gain)
        values, cotangent = gather(2), gather(3)
        k_marked = jnp.concatenate([k_ready, k_marks], axis=1)
        value_acc = key_acc = None
        attended_parts, query_parts = [], []
        for start in range(0, length, block):
            part = slice(start, start + block)
            q_block, grad_block = q_ready[part], cotangent[part]
            scores = dot(jnp.concatenate([q_block, q_marks[part]], axis=1), k_marked, (1, 1)) * (SCALE * LOG2_E)
            weights = jnp.exp2(scores)
            probs = weights * (1.0 / jnp.sum(weights, axis=1, keepdims=True))
            probs_low = probs.astype(jnp.bfloat16)
            attended = dot(probs_low, values, (1, 0)).astype(jnp.bfloat16)
            row_inner = jnp.sum(
                grad_block.astype(jnp.float32) * attended.astype(jnp.float32),
                axis=1,
                keepdims=True,
            )
            grad_probs = dot(grad_block, values, (1, 1))
            grad_scores = (probs * (grad_probs - row_inner) * SCALE).astype(jnp.bfloat16)
            value_part = dot(grad_block, probs_low, (0, 0))
            key_part = dot(q_block, grad_scores, (0, 0))
            value_acc = value_part if value_acc is None else value_acc + value_part
            key_acc = key_part if key_acc is None else key_acc + key_part
            attended_parts.append(attended)
            query_parts.append(dot(grad_scores, k_ready, (1, 0)))
        value_acc, key_acc = value_acc.T, key_acc.T
        attended = jnp.concatenate(attended_parts, axis=0)
        query_acc = jnp.concatenate(query_parts, axis=0)
        query_grad, query_sum = norm_back(query_acc, q_normed, q_inv, query_gain)
        key_grad, key_sum = norm_back(key_acc, k_normed, k_inv, key_gain)
        gain_parts = [gain_parts[0] + query_sum, gain_parts[1] + key_sum]
        results = (attended, query_grad, key_grad, value_acc.astype(jnp.bfloat16))
        for i, out in enumerate(outs):
            for t in range(TENSORS):
                out[t * rows : (t + 1) * rows, cols] = results[t][i * rows : (i + 1) * rows]
    gain_out[0:1, :] = gain_parts[0]
    gain_out[1:2, :] = gain_parts[1]


def attend(pieces, id_holders, query_gain, key_gain, rows, heads, chunk):
    groups = len(pieces)
    width = heads * HEAD_DIM
    length = groups * rows
    height = TENSORS * rows
    block = min(length, 512 if length <= 512 else 256)
    piece_spec = pl.BlockSpec((height, width), lambda i: (0, 0))
    ids_spec = pl.BlockSpec((ID_ROWS, HEAD_DIM), lambda i: (height // ID_ROWS, 0))
    gain_spec = pl.BlockSpec((1, HEAD_DIM), lambda i: (0, 0))
    area = length * length * heads
    outs = pl.pallas_call(
        functools.partial(attend_kernel, groups, rows, heads, block),
        grid=(1,),
        out_shape=[jax.ShapeDtypeStruct((height, width), jnp.bfloat16)] * groups
        + [jax.ShapeDtypeStruct((2, HEAD_DIM), jnp.float32)],
        in_specs=[piece_spec] * groups + [ids_spec] * groups + [gain_spec] * 2,
        out_specs=[piece_spec] * groups + [pl.BlockSpec((2, HEAD_DIM), lambda i: (0, 0))],
        compiler_params=pltpu.CompilerParams(vmem_limit_bytes=(24 if length <= 512 else 48) * MIB),
        cost_estimate=pl.CostEstimate(
            flops=12 * area * HEAD_DIM,
            bytes_accessed=4 * groups * height * width,
            transcendentals=area,
        ),
        name=f"attend{chunk}",
    )(*pieces, *id_holders, query_gain, key_gain)
    return list(outs[:groups]), outs[groups]


def permute(value, axis, size, shift):
    return lax.ppermute(value, axis, [(i, i ^ shift) for i in range(size)])


def add_parts_kernel(*refs):
    *parts, out = refs
    total = parts[0][...]
    for part in parts[1:]:
        total = total + part[...]
    out[...] = jnp.broadcast_to(total[None], out.shape)


def add_parts(parts, copies):
    vmem_spec = pl.BlockSpec(memory_space=pltpu.VMEM)
    return pl.pallas_call(
        add_parts_kernel,
        out_shape=jax.ShapeDtypeStruct((copies, *parts[0].shape), jnp.float32),
        in_specs=[vmem_spec] * len(parts),
        out_specs=vmem_spec,
        compiler_params=pltpu.CompilerParams(vmem_limit_bytes=4 * MIB),
        name="add_parts",
    )(*parts)


def per_device(queries, key_rows, values, cotangent, slice_ids, query_gain, key_gain):
    rows, width = queries.shape[1], queries.shape[2]
    groups, batches = lax.axis_size("seq"), lax.axis_size("dp")
    local = width // groups
    chunks = 2 if local >= 2 * HEAD_DIM else 1
    chunk_width = local // chunks
    heads = chunk_width // HEAD_DIM
    arrays = (queries, key_rows, values, cotangent)
    gains = (query_gain.reshape(1, HEAD_DIM), key_gain.reshape(1, HEAD_DIM))

    peers = list(range(1, groups))
    every = list(range(chunks))
    received = []
    for chunk in every:
        if chunk == 0:
            payloads, _ = pack(
                arrays, slice_ids, (), peers[-1:], local, chunk, chunk_width, "pack_far"
            )
            rest, gains = pack(
                arrays, slice_ids, gains, peers[:-1] + [0], local, chunk, chunk_width, "pack"
            )
            payloads.update(rest)
        else:
            payloads, _ = pack(
                arrays, None, (), peers + [0], local, chunk, chunk_width, "pack_next"
            )
        received.append(
            [payloads[0]] + [permute(payloads[shift], "seq", groups, shift) for shift in peers]
        )
    returned, gain_parts = [], []
    for chunk in range(chunks):
        results, gain_part = attend(
            received[chunk], received[0], gains[0], gains[1], rows, heads, chunk
        )
        gain_parts.append(gain_part)
        returned.append(
            [results[0]] + [permute(results[shift], "seq", groups, shift) for shift in peers]
        )
    gain_sums = lax.all_to_all(
        add_parts(gain_parts, batches * groups),
        ("dp", "seq"),
        split_axis=0,
        concat_axis=0,
        tiled=True,
    )
    early = [(returned[chunk][0], 0, chunk) for chunk in every]
    early += [(returned[chunk][s], s, chunk) for chunk in every[:-1] for s in peers]
    late = [(returned[-1][s], s, chunks - 1) for s in peers]
    outputs = unpack(early, None, None, queries.shape, local, chunk_width, "unpack")
    *outputs, query_total, key_total = unpack(
        late, gain_sums, outputs, queries.shape, local, chunk_width, "unpack_last"
    )
    return (*outputs, query_total.reshape(HEAD_DIM), key_total.reshape(HEAD_DIM))


def solution(mesh):
    rows = P("dp", "seq", None)
    return jax.shard_map(
        per_device,
        mesh=mesh,
        in_specs=(rows, rows, rows, rows, P("dp", "seq"), P(), P()),
        out_specs=(rows, rows, rows, rows, P(), P()),
        check_vma=False,
    )
```
